32 devices in a mesh: grp: 2 (over x), wid: 16 (over z, y, core).
Axes of the slice: x: 2, y: 2, z: 4, core: 2. Of those that a mesh axis runs over, the one named last changes fastest.
Arguments:
- grad_out: bfloat16 [512, 8192], P('grp', 'wid'), parts along dimension 0, may hold values from -6 to 6
- gate_saved: bfloat16 [512, 16384], P('grp', 'wid'), parts along dimension 0, may hold values from -10 to 10
- up_saved: bfloat16 [512, 16384], P('grp', 'wid'), parts along dimension 0, may hold values from -6 to 6
- w_gate: bfloat16 [8192, 16384], P(None, 'wid'), may hold values from -0.0625 to 0.0625
- w_up: bfloat16 [8192, 16384], P(None, 'wid'), may hold values from -0.0625 to 0.0625
- w_down: bfloat16 [16384, 8192], P('wid'), may hold values from -0.09375 to 0.09375
Outputs:
- grad_in: bfloat16 [512, 8192], P('grp', 'wid'), parts along dimension 0
The draws below stay inside these ranges and needn't reach their ends.
There are 2 independent parts, one for each index of `grp`. The reference program is written for one: setup_inputs(seed, part) draws one part's arguments, and reference() takes and returns one part's arrays. A program takes and returns all parts, laid end to end along the dimension named above; an argument that names none is the same for every part. Nothing has to cross between parts.
All inputs are finite; a program needn't handle non-finite values.
Results may differ from the reference program's by a relative error of at most 0.0051.
Values may be sent and summed in bfloat16 or wider, within the bound.
No kernel may reach another device: no remote copies, remote signals or barrier semaphores. Data moves between devices by JAX's collectives and lax.ppermute only.
A program may use at most 128 MiB of HBM per device.

```python
import jax
import jax.numpy as jnp
from jax import lax

D = 8192
FF = 16384
TOK = 256


def raised(drawn, key, source, target, parts, factor):
    def block_of(position):
        return (jnp.arange(drawn.shape[position]) // (drawn.shape[position] // parts)).reshape((-1,) + (1,) * (drawn.ndim - 1 - position))

    one_side = jax.random.permutation(key, parts)[block_of(target)]
    other_side = (block_of(target) + parts // 2) % parts
    return jnp.where((block_of(source) == one_side) | (block_of(source) == other_side), factor * drawn, drawn)


def levels(own_key, dims, pieces, least, largest):
    def one(dim, blocks):
        steps = jax.random.uniform(jax.random.fold_in(jax.random.fold_in(own_key, 6), dim), (blocks,), jnp.float32, least / len(pieces), largest / len(pieces))
        return jnp.repeat(jnp.exp(steps), dims[dim] // blocks).reshape((-1,) + (1,) * (len(dims) - dim - 1))

    loudness = one(*pieces[0])
    for cut in pieces[1:]:
        loudness = loudness * one(*cut)
    return loudness


def scatter_about(stream_key, dims, scale, bound, cuts=(), dtype=jnp.bfloat16):
    drawn = jax.random.normal(stream_key, dims, jnp.float32) * scale
    if len(cuts) > 0:
        drawn = levels(stream_key, dims, cuts, -0.22, 0.18) * drawn
    return jnp.clip(drawn, min=-bound, max=bound).astype(dtype)


def gaussian_with(stream_key, extent, scale, limit, split, heavy, held_as=jnp.bfloat16):
    drawn = scale * jax.random.normal(stream_key, extent, jnp.float32)
    if split:
        drawn = drawn * levels(stream_key, extent, split, -0.22, 0.18)
    return jnp.clip(raised(drawn, jax.random.fold_in(stream_key, 3), *heavy), -limit, limit).astype(held_as)


def setup_inputs(seed: int = 0, part: int = 0) -> dict:
    keys = jax.random.split(jax.random.key(seed), 7)
    part_keys = jax.random.split(jax.random.fold_in(keys[6], part), 7)
    grad_out = scatter_about(part_keys[0], (TOK, D), 1.0, 6.0, ((1, 16),))
    gate_saved = scatter_about(part_keys[1], (TOK, FF), 2.0, 10.0, ((1, 16),))
    up_saved = scatter_about(part_keys[2], (TOK, FF), 1.0, 6.0, ((1, 16),))
    w_gate = gaussian_with(keys[3], (D, FF), FF ** -0.5, 0.0625, ((1, 16),), (1, 0, 16, 2.0))
    w_up = gaussian_with(keys[4], (D, FF), FF ** -0.5, 0.0625, ((1, 16),), (1, 0, 16, 2.0))
    w_down = gaussian_with(keys[5], (FF, D), D ** -0.5, 0.09375, ((0, 16),), (1, 0, 16, 2.0))
    return dict(grad_out=grad_out, gate_saved=gate_saved, up_saved=up_saved, w_gate=w_gate, w_up=w_up, w_down=w_down)


def reference(grad_out, gate_saved, up_saved, w_gate, w_up, w_down):
    grad_hidden = lax.dot_general(grad_out, w_down, (((1,), (1,)), ((), ())), preferred_element_type=jnp.float32)
    gate = gate_saved.astype(jnp.float32)
    up = up_saved.astype(jnp.float32)
    sig = jax.nn.sigmoid(gate)
    grad_gate = (grad_hidden * up * sig * (1.0 + gate * (1.0 - sig))).astype(jnp.bfloat16)
    grad_up = (grad_hidden * gate * sig).astype(jnp.bfloat16)
    total = lax.dot_general(grad_gate, w_gate, (((1,), (1,)), ((), ())), preferred_element_type=jnp.float32)
    total = total + lax.dot_general(grad_up, w_up, (((1,), (1,)), ((), ())), preferred_element_type=jnp.float32)
    return total.astype(jnp.bfloat16)
```

```python
import functools

import jax
import jax.numpy as jnp
from jax import lax
from jax.experimental import pallas as pl
from jax.experimental.pallas import tpu as pltpu
from jax.sharding import PartitionSpec as P

BF16, F32 = jnp.bfloat16, jnp.float32
TILE = 256
VMEM = 24 * 2**20


def contract_last(left, right):
    return lax.dot_general(
        left, right, (((1,), (1,)), ((), ())), preferred_element_type=F32
    )


def call(body, blocks, grid, ins, outs, args, flops, read):
    return pl.pallas_call(
        body,
        grid_spec=pltpu.PrefetchScalarGridSpec(
            num_scalar_prefetch=1,
            grid=(grid,),
            in_specs=[pl.BlockSpec(shape, index) for shape, index in ins],
            out_specs=[pl.BlockSpec(shape, index) for shape, index, _ in outs],
        ),
        out_shape=[out for _, _, out in outs],
        compiler_params=pltpu.CompilerParams(vmem_limit_bytes=VMEM),
        cost_estimate=pl.CostEstimate(
            flops=flops, bytes_accessed=read, transcendentals=0
        ),
    )(blocks, *args)


def whole(i, b):
    return 0, 0


def column(i, b):
    return 0, i


def factors_body(blocks, gate_ref, up_ref, to_gate_ref, to_up_ref):
    gate = gate_ref[...].astype(F32)
    up = up_ref[...].astype(F32)
    sig = jax.nn.sigmoid(gate)
    to_gate_ref[...] = up * sig * (1.0 + gate * (1.0 - sig))
    to_up_ref[...] = gate * sig


def factors(blocks, gate, up):
    tok, ff = gate.shape
    spec = ((tok, TILE), column)
    out = (*spec, jax.ShapeDtypeStruct((tok, ff), F32))
    return call(factors_body, blocks, ff // TILE, [spec] * 2, [out] * 2, (gate, up), 0, 12 * tok * ff)


def hidden_body(parts, first, last, blocks, *refs):
    pieces, weights, rest = refs[:parts], refs[parts : 2 * parts], list(refs[2 * parts :])
    total = 0.0 if first else rest.pop(0)[...]
    for piece, weight in zip(pieces, weights):
        total = total + contract_last(piece[...], weight[...])
    if last:
        to_gate, to_up, grad_gate, grad_up = rest
        grad_gate[...] = (total * to_gate[...]).astype(BF16)
        grad_up[...] = (total * to_up[...]).astype(BF16)
    else:
        rest[0][...] = total


def hidden(blocks, pieces, w_down, total=None, scale=None):
    tok, width = pieces[0].shape
    ff = w_down.shape[0]
    parts = len(pieces)
    tile = ((tok, TILE), column)
    ins = [((tok, width), whole)] * parts
    ins += [((TILE, width), lambda i, b, j=j: (i, b[j])) for j in range(parts)]
    args = (*pieces, *([w_down] * parts))
    if total is not None:
        ins, args = ins + [tile], (*args, total)
    if scale is not None:
        ins, args = ins + [tile] * 2, (*args, *scale)
        outs = [(*tile, jax.ShapeDtypeStruct((tok, ff), BF16))] * 2
    else:
        outs = [(*tile, jax.ShapeDtypeStruct((tok, ff), F32))]
    body = functools.partial(hidden_body, parts, total is None, scale is not None)
    done = call(body, blocks, ff // TILE, ins, outs, args, 2 * parts * tok * width * ff, 2 * parts * width * ff)
    return done if scale is not None else done[0]


def partial_sum(grad_gate, grad_up, w_gate, w_up):
    return contract_last(grad_gate[...], w_gate[...]) + contract_last(grad_up[...], w_up[...])


def send_body(blocks, grad_gate, grad_up, w_gate, w_up, out):
    out[...] = partial_sum(grad_gate, grad_up, w_gate, w_up).astype(BF16)


def keep_body(half, blocks, grad_gate, grad_up, w_gate, w_up, got, keep, send):
    total = partial_sum(grad_gate, grad_up, w_gate, w_up) + got[...].astype(F32)
    i = pl.program_id(0)

    @pl.when(i < half)
    def _():
        send[...] = total.astype(BF16)

    @pl.when(i >= half)
    def _():
        keep[...] = total


def rows(per):
    return lambda i, b: (b[i // per] * per + i % per, 0)


def send_parts(blocks, grads, weights, width):
    tok, ff = grads[0].shape
    per = width // TILE
    ins = [((tok, ff), whole)] * 2 + [((TILE, ff), rows(per))] * 2
    outs = [((tok, TILE), column, jax.ShapeDtypeStruct((tok, 2 * width), BF16))]
    return call(send_body, blocks, 2 * per, ins, outs, (*grads, *weights), 8 * tok * ff * width, 8 * ff * width)[0]


def keep_parts(blocks, grads, weights, got, width):
    tok, ff = grads[0].shape
    per = width // TILE
    ins = [((tok, ff), whole)] * 2 + [((TILE, ff), rows(per))] * 2 + [((tok, TILE), column)]
    outs = [
        ((tok, TILE), lambda i, b: (0, jnp.maximum(i - per, 0)), jax.ShapeDtypeStruct((tok, width), F32)),
        ((tok, TILE), lambda i, b: (0, jnp.minimum(i, per - 1)), jax.ShapeDtypeStruct((tok, width), BF16)),
    ]
    body = functools.partial(keep_body, per)
    return call(body, blocks, 2 * per, ins, outs, (*grads, *weights, got), 8 * tok * ff * width, 8 * ff * width)


def staged(grad_out, gate_saved, up_saved, w_gate, w_up, w_down):
    n = 16
    width = grad_out.shape[1]
    me = lax.axis_index("wid")
    line, row, pair = me // 4, (me // 2) % 2, me % 2
    places = {
        "own": line,
        "near": line ^ 1,
        "mid": jnp.where(line < 2, 2, 1),
        "far": jnp.where(line < 2, 3, 0),
    }

    def blocks(name, order):
        first = 4 * places[name]
        return jnp.stack([first + 2 * (row ^ r) + (pair ^ p) for r, p in order]).astype(jnp.int32)

    pairs = [(i, i ^ 1) for i in range(n)]
    rows_ = [(i, i ^ 2) for i in range(n)]
    outer = [(i, i ^ 4) for i in range(n)]
    inner = [(i, i + 4) for i in range(4, 8)] + [(i, i - 4) for i in range(8, 12)]
    outward = [(i, i - 4) for i in range(4, 8)] + [(i, i + 4) for i in range(8, 12)]
    inward = [(j, i) for i, j in outward]
    is_mid = (line == 1) | (line == 2)

    def move(x, perm):
        return lax.ppermute(x, "wid", perm)

    scale = factors(blocks("own", [(0, 0)]), gate_saved, up_saved)

    held = {"own": grad_out}
    held["near"] = move(grad_out, outer)
    mid = move(grad_out, inner)
    far = move(held["near"], inner)
    held["mid"] = mid + move(mid, outward)
    held["far"] = far + move(far, outward)

    order = [(0, 0), (0, 1), (1, 0), (1, 1)]
    total = None
    for name in ("own", "near", "mid", "far"):
        here = held[name]
        across = move(here, rows_)
        pieces = [here, move(here, pairs), across, move(across, pairs)]
        last = name == "far"
        total = hidden(blocks(name, order), pieces, w_down, total, scale if last else None)
    grads, weights = total, (w_gate, w_up)

    kept = {}
    for name in ("far", "mid", "near", "own"):
        sent = send_parts(blocks(name, [(1, 1), (0, 1)]), grads, weights, width)
        got = move(sent, pairs)
        keep, across = keep_parts(blocks(name, [(1, 0), (0, 0)]), grads, weights, got, width)
        kept[name] = keep + move(across, rows_).astype(F32)

    far = kept["far"] + move(kept["far"].astype(BF16), inward).astype(F32)
    near = kept["near"] + move(far.astype(BF16), inner).astype(F32)
    mid = kept["mid"] + move(kept["mid"].astype(BF16), inward).astype(F32)
    own = kept["own"] + move(mid.astype(BF16), inner).astype(F32)
    own = own + move(near.astype(BF16), outer).astype(F32)
    return own.astype(BF16)


def local(grad_out, gate_saved, up_saved, w_gate, w_up, w_down):
    grad_hidden = contract_last(lax.all_gather(grad_out, "wid", axis=1, tiled=True), w_down)
    gate = gate_saved.astype(F32)
    up = up_saved.astype(F32)
    sig = jax.nn.sigmoid(gate)
    grad_gate = (grad_hidden * up * sig * (1.0 + gate * (1.0 - sig))).astype(BF16)
    grad_up = (grad_hidden * gate * sig).astype(BF16)
    summed = lax.psum_scatter(
        contract_last(w_gate, grad_gate) + contract_last(w_up, grad_up),
        "wid",
        scatter_dimension=0,
        tiled=True,
    )
    return summed.astype(BF16).T


def solution(mesh):
    in_specs = (
        P("grp", "wid"),
        P("grp", "wid"),
        P("grp", "wid"),
        P(None, "wid"),
        P(None, "wid"),
        P("wid", None),
    )
    out_specs = P("grp", "wid")
    body = staged if mesh.shape["wid"] == 16 else local
    return jax.shard_map(body, mesh=mesh, in_specs=in_specs, out_specs=out_specs, check_vma=False)
```

```python
import functools

import jax
import jax.numpy as jnp
from jax import lax
from jax.experimental import pallas as pl
from jax.experimental.pallas import tpu as pltpu
from jax.sharding import PartitionSpec as P

BF16, F32 = jnp.bfloat16, jnp.float32
TILE = 256
VMEM = 16 * 2**20


def contract_last(left, right):
    return lax.dot_general(
        left, right, (((1,), (1,)), ((), ())), preferred_element_type=F32
    )


def call(body, blocks, ins, outs, args, scratch, micros):
    return pl.pallas_call(
        body,
        in_specs=[pl.BlockSpec(memory_space=space) for space in (pltpu.SMEM, *ins)],
        out_specs=[pl.BlockSpec(memory_space=pltpu.VMEM) for _ in outs],
        out_shape=outs,
        scratch_shapes=scratch,
        compiler_params=pltpu.CompilerParams(vmem_limit_bytes=VMEM),
        cost_estimate=pl.CostEstimate(flops=int(micros * 1e9), bytes_accessed=0, transcendentals=0),
    )(blocks, *args)


class Ahead:
    def __init__(self, blocks, first, weights, outs, sem):
        self.blocks, self.first, self.weights, self.outs, self.sem = blocks, first, weights, outs, sem
        self.width = outs[0].shape[0] // 4

    def copies(self, j):
        source = pl.ds(pl.multiple_of(self.blocks[self.first + j] * self.width, self.width), self.width)
        at = pl.ds(j * self.width, self.width)
        return [
            pltpu.make_async_copy(weight.at[source], out.at[at], self.sem.at[k, j])
            for k, (weight, out) in enumerate(zip(self.weights, self.outs))
        ]

    def start(self):
        for j in range(4):
            for copy in self.copies(j):
                copy.start()

    def wait(self):
        for j in range(4):
            for copy in self.copies(j):
                copy.wait()


def factors_body(
    blocks, gate, up, w_gate, w_up, to_gate_ref, to_up_ref, ahead_gate, ahead_up, gate_ref, up_ref, saved_sem, sem
):
    saved = [
        pltpu.make_async_copy(source, to, saved_sem.at[k])
        for k, (source, to) in enumerate([(gate, gate_ref), (up, up_ref)])
    ]
    for copy in saved:
        copy.start()
    ahead = Ahead(blocks, 0, (w_gate, w_up), (ahead_gate, ahead_up), sem)
    ahead.start()
    for copy in saved:
        copy.wait()

    def step(i, carry):
        at = pl.ds(pl.multiple_of(i * 32, 32), 32)
        gate = gate_ref[at].astype(F32)
        up = up_ref[at].astype(F32)
        sig = jax.nn.sigmoid(gate)
        to_gate_ref[at] = up * sig * (1.0 + gate * (1.0 - sig))
        to_up_ref[at] = gate * sig
        return carry

    lax.fori_loop(0, gate_ref.shape[0] // 32, step, 0)
    ahead.wait()


def held_weights(weights, width):
    return [pltpu.VMEM((4 * width, weight.shape[1]), BF16) for weight in weights]


def factors(blocks, gate, up, weights, width):
    tok, ff = gate.shape
    outs = [jax.ShapeDtypeStruct((tok, ff), F32)] * 2 + held_weights(weights, width)
    ins = [pl.ANY] * 4
    scratch = [pltpu.VMEM((tok, ff), BF16)] * 2 + [pltpu.SemaphoreType.DMA((2,)), pltpu.SemaphoreType.DMA((2, 4))]
    *scale, ahead_gate, ahead_up = call(factors_body, blocks, ins, outs, (gate, up, *weights), scratch, 4.0)
    return scale, (ahead_gate, ahead_up)


def hidden_body(parts, first, last, fetch, blocks, *refs):
    refs = list(refs)
    pieces, w_down, rest = refs[:parts], refs[parts], refs[parts + 1 :]
    ahead_sem = rest.pop() if fetch else None
    piece_sem, weight_sem = rest.pop(), rest.pop()
    held, weights = rest.pop(), rest.pop()
    if fetch:
        outs = [rest.pop(), rest.pop()][::-1]
        ahead = Ahead(blocks, parts, [rest.pop(0), rest.pop(0)], outs, ahead_sem)
    before = None if first else rest.pop(0)
    width = pieces[0].shape[1]
    count = w_down.shape[0] // TILE

    def arrival(j):
        return pltpu.make_async_copy(pieces[j], held.at[:, pl.ds(j * width, width)], piece_sem.at[j])

    def weight(i, j):
        at = pl.ds(pl.multiple_of(i * TILE, TILE), TILE)
        source = pl.ds(pl.multiple_of(blocks[j] * width, width), width)
        return pltpu.make_async_copy(
            w_down.at[at, source], weights.at[at, pl.ds(j * width, width)], weight_sem.at[i, j]
        )

    def start(i, carry):
        for j in range(parts):
            weight(i, j).start()
        return carry

    for j in range(parts):
        arrival(j).start()
    lax.fori_loop(0, count, start, 0)
    if fetch:
        ahead.start()
    for j in range(parts):
        arrival(j).wait()

    def step(i, carry):
        for j in range(parts):
            weight(i, j).wait()
        at = pl.ds(pl.multiple_of(i * TILE, TILE), TILE)
        total = contract_last(held[...], weights[at])
        if not first:
            total = total + before[:, at]
        if last:
            to_gate, to_up, grad_gate, grad_up = rest
            grad_gate[:, at] = (total * to_gate[:, at]).astype(BF16)
            grad_up[:, at] = (total * to_up[:, at]).astype(BF16)
        else:
            rest[0][:, at] = total
        return carry

    lax.fori_loop(0, count, step, 0)
    if fetch:
        ahead.wait()


def hidden(blocks, pieces, w_down, total=None, scale=None, fetch=None):
    tok, width = pieces[0].shape
    ff = w_down.shape[0]
    parts = len(pieces)
    ins, args = [pl.ANY] * (parts + 1), (*pieces, w_down)
    if fetch is not None:
        ins, args = ins + [pl.ANY] * 2, (*args, *fetch)
    if total is not None:
        ins, args = ins + [pltpu.VMEM], (*args, total)
    if scale is not None:
        ins, args = ins + [pltpu.VMEM] * 2, (*args, *scale)
        outs = [jax.ShapeDtypeStruct((tok, ff), BF16)] * 2
    else:
        outs = [jax.ShapeDtypeStruct((tok, ff), F32)]
    scratch = [
        pltpu.VMEM((ff, parts * width), BF16),
        pltpu.VMEM((tok, parts * width), BF16),
        pltpu.SemaphoreType.DMA((ff // TILE, parts)),
        pltpu.SemaphoreType.DMA((parts,)),
    ]
    if fetch is not None:
        outs += held_weights(fetch, width)
        scratch.append(pltpu.SemaphoreType.DMA((2, 4)))
    body = functools.partial(hidden_body, parts, total is None, scale is not None, fetch is not None)
    done = call(body, blocks, ins, outs, args, scratch, 5.0 if fetch is not None else 3.0)
    return done


def partial_sum(at, grad_gate, grad_up, w_gate, w_up):
    return contract_last(grad_gate[...], w_gate[at]) + contract_last(grad_up[...], w_up[at])


def send_body(width, grad_gate, grad_up, w_gate, w_up, out):
    def step(i, carry):
        at = pl.ds(pl.multiple_of(i * width, width), width)
        out[:, at] = partial_sum(at, grad_gate, grad_up, w_gate, w_up).astype(BF16)
        return carry

    lax.fori_loop(0, 2, step, 0)


def keep_body(width, grad_gate, grad_up, w_gate, w_up, got, keep, send):
    def step(i, carry):
        here = pl.ds(pl.multiple_of(i * width, width), width)
        at = pl.ds(pl.multiple_of((2 + i) * width, width), width)
        total = partial_sum(at, grad_gate, grad_up, w_gate, w_up) + got[:, here].astype(F32)

        @pl.when(i == 0)
        def _():
            send[...] = total.astype(BF16)

        @pl.when(i == 1)
        def _():
            keep[...] = total

        return carry

    lax.fori_loop(0, 2, step, 0)


def plain(body, args, outs, micros):
    spec = pl.BlockSpec(memory_space=pltpu.VMEM)
    return pl.pallas_call(
        body,
        in_specs=[spec] * len(args),
        out_specs=[spec] * len(outs),
        out_shape=[jax.ShapeDtypeStruct(*out) for out in outs],
        compiler_params=pltpu.CompilerParams(vmem_limit_bytes=VMEM),
        cost_estimate=pl.CostEstimate(flops=int(micros * 1e9), bytes_accessed=0, transcendentals=0),
    )(*args)


def send_parts(grads, weights, width):
    outs = [((grads[0].shape[0], 2 * width), BF16)]
    return plain(functools.partial(send_body, width), (*grads, *weights), outs, 2.0)[0]


def keep_parts(grads, weights, got, width):
    tok = grads[0].shape[0]
    outs = [((tok, width), F32), ((tok, width), BF16)]
    return plain(functools.partial(keep_body, width), (*grads, *weights, got), outs, 2.0)


def staged(grad_out, gate_saved, up_saved, w_gate, w_up, w_down):
    n = 16
    width = grad_out.shape[1]
    me = lax.axis_index("wid")
    line, row, pair = me // 4, (me // 2) % 2, me % 2
    places = {
        "own": line,
        "near": line ^ 1,
        "mid": jnp.where(line < 2, 2, 1),
        "far": jnp.where(line < 2, 3, 0),
    }

    def blocks(*wanted):
        return jnp.stack(
            [4 * places[name] + 2 * (row ^ r) + (pair ^ p) for name, order in wanted for r, p in order]
        ).astype(jnp.int32)

    pairs = [(i, i ^ 1) for i in range(n)]
    rows = [(i, i ^ 2) for i in range(n)]
    outer = [(i, i ^ 4) for i in range(n)]
    inner = [(i, i + 4) for i in range(4, 8)] + [(i, i - 4) for i in range(8, 12)]
    outward = [(i, i - 4) for i in range(4, 8)] + [(i, i + 4) for i in range(8, 12)]
    inward = [(j, i) for i, j in outward]

    def move(x, perm):
        return lax.ppermute(x, "wid", perm)

    in_hbm = functools.partial(pltpu.with_memory_space_constraint, memory_space=pltpu.HBM)
    gate_saved, up_saved, w_gate, w_up, w_down = map(in_hbm, (gate_saved, up_saved, w_gate, w_up, w_down))
    weights = (w_gate, w_up)
    arriving = [(0, 0), (0, 1), (1, 0), (1, 1)]
    leaving = [(1, 1), (0, 1), (1, 0), (0, 0)]
    ahead = {}
    scale, ahead["own"] = factors(blocks(("own", leaving)), gate_saved, up_saved, weights, width)

    near = move(grad_out, outer)
    mid = move(grad_out, inner)
    own_row = move(grad_out, rows)
    own_pair = move(grad_out, pairs)

    far = move(near, inner)
    mid = mid + move(mid, outward)
    near_row = move(near, rows)
    near_pair = move(near, pairs)
    own_both = move(own_row, pairs)
    total, *ahead["near"] = hidden(
        blocks(("own", arriving), ("near", leaving)), [grad_out, own_pair, own_row, own_both], w_down, fetch=weights
    )

    far = far + move(far, outward)
    mid_row = move(mid, rows)
    mid_pair = move(mid, pairs)
    near_both = move(near_row, pairs)
    total, *ahead["mid"] = hidden(
        blocks(("near", arriving), ("mid", leaving)), [near, near_pair, near_row, near_both], w_down, total, fetch=weights
    )

    far_row = move(far, rows)
    far_pair = move(far, pairs)
    mid_both = move(mid_row, pairs)
    total, *ahead["far"] = hidden(
        blocks(("mid", arriving), ("far", arriving[:2] + leaving)),
        [mid, mid_pair, mid_row, mid_both, far, far_pair], w_down, total, fetch=weights,
    )

    far_both = move(far_row, pairs)
    grads = hidden(blocks(("far", arriving[2:])), [far_row, far_both], w_down, total, scale)

    kept = {}
    for name in ("far", "mid", "near", "own"):
        got = move(send_parts(grads, ahead[name], width), pairs)
        keep, across = keep_parts(grads, ahead[name], got, width)
        kept[name] = keep + move(across, rows).astype(F32)

    far = kept["far"] + move(kept["far"].astype(BF16), inward).astype(F32)
    near = kept["near"] + move(far.astype(BF16), inner).astype(F32)
    mid = kept["mid"] + move(kept["mid"].astype(BF16), inward).astype(F32)
    own = kept["own"] + move(mid.astype(BF16), inner).astype(F32)
    own = own + move(near.astype(BF16), outer).astype(F32)
    return own.astype(BF16)


def local(grad_out, gate_saved, up_saved, w_gate, w_up, w_down):
    grad_hidden = contract_last(lax.all_gather(grad_out, "wid", axis=1, tiled=True), w_down)
    gate = gate_saved.astype(F32)
    up = up_saved.astype(F32)
    sig = jax.nn.sigmoid(gate)
    grad_gate = (grad_hidden * up * sig * (1.0 + gate * (1.0 - sig))).astype(BF16)
    grad_up = (grad_hidden * gate * sig).astype(BF16)
    summed = lax.psum_scatter(
        contract_last(w_gate, grad_gate) + contract_last(w_up, grad_up),
        "wid",
        scatter_dimension=0,
        tiled=True,
    )
    return summed.astype(BF16).T


def solution(mesh):
    in_specs = (
        P("grp", "wid"),
        P("grp", "wid"),
        P("grp", "wid"),
        P(None, "wid"),
        P(None, "wid"),
        P("wid", None),
    )
    out_specs = P("grp", "wid")
    body = staged if mesh.shape["wid"] == 16 else local
    return jax.shard_map(body, mesh=mesh, in_specs=in_specs, out_specs=out_specs, check_vma=False)
```

```python
import functools

import jax
import jax.numpy as jnp
from jax import lax
from jax.experimental import pallas as pl
from jax.experimental.pallas import tpu as pltpu
from jax.sharding import PartitionSpec as P

BF16, F32 = jnp.bfloat16, jnp.float32
TILE = 256
VMEM = 10 * 2**20
COST = 2e8


def contract_last(left, right):
    return lax.dot_general(
        left, right, (((1,), (1,)), ((), ())), preferred_element_type=F32
    )


OWN, NEAR, MID, FAR = range(4)


def shard(place, row, pair):
    return lax.axis_index("wid") ^ (4 * place + 2 * row + pair)


def call(body, ins, outs, args, scratch, micros):
    return pl.pallas_call(
        body,
        in_specs=[pl.BlockSpec(memory_space=space) for space in ins],
        out_specs=[pl.BlockSpec(memory_space=pltpu.VMEM) for _ in outs],
        out_shape=outs,
        scratch_shapes=scratch,
        compiler_params=pltpu.CompilerParams(vmem_limit_bytes=VMEM),
        cost_estimate=pl.CostEstimate(flops=int(micros * COST), bytes_accessed=0, transcendentals=0),
    )(*args)


def factors_body(gate, up, to_gate_ref, to_up_ref, gate_ref, up_ref, sem):
    copies = [
        pltpu.make_async_copy(source, to, sem.at[k])
        for k, (source, to) in enumerate([(gate, gate_ref), (up, up_ref)])
    ]
    for copy in copies:
        copy.start()
    for copy in copies:
        copy.wait()

    def step(i, carry):
        at = pl.ds(pl.multiple_of(i * 32, 32), 32)
        gate = gate_ref[at].astype(F32)
        up = up_ref[at].astype(F32)
        sig = jax.nn.sigmoid(gate)
        to_gate_ref[at] = up * sig * (1.0 + gate * (1.0 - sig))
        to_up_ref[at] = gate * sig
        return carry

    lax.fori_loop(0, gate_ref.shape[0] // 32, step, 0)


def factors(gate, up):
    tok, ff = gate.shape
    outs = [jax.ShapeDtypeStruct((tok, ff), F32)] * 2
    scratch = [pltpu.VMEM((tok, ff), BF16)] * 2 + [pltpu.SemaphoreType.DMA((2,))]
    return call(factors_body, [pl.ANY] * 2, outs, (gate, up), scratch, 1.0)


def hidden_body(shards, first, last, soon, *refs):
    refs, parts = list(refs), len(shards)
    blocks = [shard(*which) for which in shards]
    pieces, w_down, rest = refs[:parts], refs[parts], refs[parts + 1 :]
    piece_sem, weight_sem = rest.pop(), rest.pop()
    held, weights = rest.pop(), rest.pop()
    width = pieces[0].shape[1]
    before = None if first else rest.pop(0)
    if soon:
        del rest[2 * last : 2 * last + soon]
    count = w_down.shape[0] // TILE

    def arrival(j):
        return pltpu.make_async_copy(pieces[j], held.at[:, pl.ds(j * width, width)], piece_sem.at[j])

    def weight(i, j):
        at = pl.ds(pl.multiple_of(i * TILE, TILE), TILE)
        source = pl.ds(pl.multiple_of(blocks[j] * width, width), width)
        return pltpu.make_async_copy(
            w_down.at[at, source], weights.at[at, pl.ds(j * width, width)], weight_sem.at[i, j]
        )

    def start(i, carry):
        for j in range(parts):
            weight(i, j).start()
        return carry

    for j in range(parts):
        arrival(j).start()
    lax.fori_loop(0, count, start, 0)
    for j in range(parts):
        arrival(j).wait()

    def step(i, carry):
        for j in range(parts):
            weight(i, j).wait()
        at = pl.ds(pl.multiple_of(i * TILE, TILE), TILE)
        total = contract_last(held[...], weights[at])
        if not first:
            total = total + before[:, at]
        if last:
            to_gate, to_up, grad_gate, grad_up = rest
            grad_gate[:, at] = (total * to_gate[:, at]).astype(BF16)
            grad_up[:, at] = (total * to_up[:, at]).astype(BF16)
        else:
            rest[0][:, at] = total
        return carry

    lax.fori_loop(0, count, step, 0)


def hidden(pieces, w_down, total=None, scale=None, soon=()):
    shards, pieces = zip(*pieces)
    tok, width = pieces[0].shape
    ff = w_down.shape[0]
    parts = len(pieces)
    ins, args = [pl.ANY] * (parts + 1), (*pieces, w_down)
    if total is not None:
        ins, args = ins + [pltpu.VMEM], (*args, total)
    if scale is not None:
        ins, args = ins + [pltpu.VMEM] * 2, (*args, *scale)
        outs = [jax.ShapeDtypeStruct((tok, ff), BF16)] * 2
    else:
        outs = [jax.ShapeDtypeStruct((tok, ff), F32)]
    ins, args = ins + [pltpu.VMEM] * len(soon), (*args, *soon)
    scratch = [
        pltpu.VMEM((ff, parts * width), BF16),
        pltpu.VMEM((tok, parts * width), BF16),
        pltpu.SemaphoreType.DMA((ff // TILE, parts)),
        pltpu.SemaphoreType.DMA((parts,)),
    ]
    body = functools.partial(hidden_body, shards, total is None, scale is not None, len(soon))
    return call(body, ins, outs, args, scratch, 3.0)


def partial_sum(block, width, grad_gate, grad_up, w_gate, w_up):
    at = pl.ds(pl.multiple_of(block * width, width), width)
    return contract_last(grad_gate[...], w_gate[at]) + contract_last(grad_up[...], w_up[at])


def each_row(width, body):
    def step(i, carry):
        body(i, pl.ds(pl.multiple_of(i * width, width), width))
        return carry

    lax.fori_loop(0, 2, step, 0)


def sums_body(kept, sent, width, grad_gate, grad_up, w_gate, w_up, *refs):
    given = (grad_gate, grad_up, w_gate, w_up)
    refs = list(refs)
    if kept is not None:
        got, keep, cross = refs.pop(0), refs.pop(0), refs.pop(0)

        def keep_row(i, at):
            total = partial_sum(shard(kept, 1 - i, 0), width, *given) + got[:, at].astype(F32)

            @pl.when(i == 0)
            def _():
                cross[...] = total.astype(BF16)

            @pl.when(i == 1)
            def _():
                keep[...] = total

        each_row(width, keep_row)
    if sent is not None:
        out = refs.pop(0)

        def send_row(i, at):
            out[:, at] = partial_sum(shard(sent, 1 - i, 1), width, *given).astype(BF16)

        each_row(width, send_row)


def sums(grads, weights, width, kept=None, got=None, sent=None):
    tok = grads[0].shape[0]
    args, outs = (*grads, *weights), []
    if kept is not None:
        args = (*args, got)
        outs += [jax.ShapeDtypeStruct((tok, width), F32), jax.ShapeDtypeStruct((tok, width), BF16)]
    if sent is not None:
        outs += [jax.ShapeDtypeStruct((tok, 2 * width), BF16)]
    body = functools.partial(sums_body, kept, sent, width)
    return call(body, [pltpu.VMEM] * len(args), outs, args, [], 1.5 * len(outs) / 2)


def after(x, *earlier):
    return lax.optimization_barrier((x, *earlier))[0]


def staged(grad_out, gate_saved, up_saved, w_gate, w_up, w_down):
    n = 16
    width = grad_out.shape[1]

    def move(x, bits):
        return lax.ppermute(x, "wid", [(i, i ^ bits) for i in range(n)])

    pair, row, near_, mid_ = 1, 2, 4, 8
    half = grad_out.shape[0] // 2
    in_hbm = functools.partial(pltpu.with_memory_space_constraint, memory_space=pltpu.HBM)
    gate_saved, up_saved, w_down = map(in_hbm, (gate_saved, up_saved, w_down))
    weights = [pltpu.with_memory_space_constraint(w, pltpu.VMEM) for w in (w_gate, w_up)]

    scale = factors(gate_saved, up_saved)
    own_row = move(grad_out, row)
    near = move(grad_out, near_)
    mid_a = move(grad_out[:half], mid_)
    own_pair = move(grad_out, pair)

    near = after(near, scale[0])
    near_row = move(near, row)
    mid_b = move(after(grad_out[half:], near), mid_)
    far_a = move(mid_a, near_)
    near_pair = move(near, pair)
    own_both = move(own_row, pair)
    (total,) = hidden(
        [((OWN, 0, 0), in_hbm(grad_out)), ((OWN, 0, 1), own_pair), ((OWN, 1, 0), own_row), ((NEAR, 0, 0), near)], w_down
    )

    mid_b, near_row = after(mid_b, total, near_row), after(near_row, mid_b)
    mid = jnp.concatenate([mid_a, mid_b])
    mid_row = move(mid, row)
    far_b = move(mid_b, near_)
    mid_pair = move(mid, pair)
    near_both = move(near_row, pair)
    (total,) = hidden(
        [((OWN, 1, 1), own_both), ((NEAR, 0, 1), near_pair), ((NEAR, 1, 0), near_row), ((MID, 0, 0), mid)], w_down, total
    )

    far_b = after(far_b, total)
    far = jnp.concatenate([far_a, far_b])
    far_row = move(far, row)
    far_pair = move(far, pair)
    mid_both = move(mid_row, pair)
    (total,) = hidden(
        [
            ((NEAR, 1, 1), near_both),
            ((MID, 0, 1), mid_pair),
            ((MID, 1, 0), mid_row),
            ((FAR, 0, 0), far),
            ((MID, 1, 1), mid_both),
            ((FAR, 0, 1), far_pair),
        ],
        w_down,
        total,
        soon=weights,
    )

    far_row = after(far_row, total)
    far_both = move(far_row, pair)
    grads = hidden([((FAR, 1, 0), far_row), ((FAR, 1, 1), far_both)], w_down, total, scale)

    step = functools.partial(sums, grads, weights, width)
    (sent_far,) = step(sent=FAR)
    (sent_mid,) = step(sent=MID)
    far, cross_far = step(kept=FAR, got=move(sent_far, pair))
    mid, cross_mid, sent_near = step(kept=MID, got=move(sent_mid, pair), sent=NEAR)
    far = far + move(cross_far, row).astype(F32)

    near, cross_near, sent_own = step(kept=NEAR, got=move(sent_near, pair), sent=OWN)
    mid = mid + after(move(cross_mid, row), cross_near).astype(F32) + move(far.astype(BF16), near_).astype(F32)

    own, cross_own = step(kept=OWN, got=move(sent_own, pair))
    mid = mid.astype(BF16)
    mid_a, near_row = move(mid[:half], mid_), move(cross_near, row)
    mid_a, near_row = after(mid_a, near_row, cross_own), after(near_row, mid_a, cross_own)
    near = near + near_row.astype(F32)

    near = move(near.astype(BF16), near_)
    mid_b = move(mid[half:], mid_)
    own = own + move(cross_own, row).astype(F32) + jnp.concatenate([mid_a, mid_b]).astype(F32)
    return (after(own) + near.astype(F32)).astype(BF16)


def local(grad_out, gate_saved, up_saved, w_gate, w_up, w_down):
    grad_hidden = contract_last(lax.all_gather(grad_out, "wid", axis=1, tiled=True), w_down)
    gate = gate_saved.astype(F32)
    up = up_saved.astype(F32)
    sig = jax.nn.sigmoid(gate)
    grad_gate = (grad_hidden * up * sig * (1.0 + gate * (1.0 - sig))).astype(BF16)
    grad_up = (grad_hidden * gate * sig).astype(BF16)
    summed = lax.psum_scatter(
        contract_last(w_gate, grad_gate) + contract_last(w_up, grad_up),
        "wid",
        scatter_dimension=0,
        tiled=True,
    )
    return summed.astype(BF16).T


def solution(mesh):
    in_specs = (
        P("grp", "wid"),
        P("grp", "wid"),
        P("grp", "wid"),
        P(None, "wid"),
        P(None, "wid"),
        P("wid", None),
    )
    out_specs = P("grp", "wid")
    body = staged if mesh.shape["wid"] == 16 else local
    return jax.shard_map(body, mesh=mesh, in_specs=in_specs, out_specs=out_specs, check_vma=False)
```

```python
import functools

import jax
import jax.numpy as jnp
from jax import lax
from jax.experimental import pallas as pl
from jax.experimental.pallas import tpu as pltpu
from jax.sharding import PartitionSpec as P

BF16, F32 = jnp.bfloat16, jnp.float32
TILE = 256
VMEM = 10 * 2**20
COST = 2e8


def contract_last(left, right):
    return lax.dot_general(
        left, right, (((1,), (1,)), ((), ())), preferred_element_type=F32
    )


OWN, NEAR, MID, FAR = range(4)


def shard(place, row, pair):
    return lax.axis_index("wid") ^ (4 * place + 2 * row + pair)


def call(body, ins, outs, args, scratch, micros):
    return pl.pallas_call(
        body,
        in_specs=[pl.BlockSpec(memory_space=space) for space in ins],
        out_specs=[pl.BlockSpec(memory_space=pltpu.VMEM) for _ in outs],
        out_shape=outs,
        scratch_shapes=scratch,
        compiler_params=pltpu.CompilerParams(vmem_limit_bytes=VMEM),
        cost_estimate=pl.CostEstimate(flops=int(micros * COST), bytes_accessed=0, transcendentals=0),
    )(*args)


def factors_body(gate, up, to_gate_ref, to_up_ref, gate_ref, up_ref, sem):
    copies = [
        pltpu.make_async_copy(source, to, sem.at[k])
        for k, (source, to) in enumerate([(gate, gate_ref), (up, up_ref)])
    ]
    for copy in copies:
        copy.start()
    for copy in copies:
        copy.wait()

    def step(i, carry):
        at = pl.ds(pl.multiple_of(i * 32, 32), 32)
        gate = gate_ref[at].astype(F32)
        up = up_ref[at].astype(F32)
        sig = jax.nn.sigmoid(gate)
        to_gate_ref[at] = up * sig * (1.0 + gate * (1.0 - sig))
        to_up_ref[at] = gate * sig
        return carry

    lax.fori_loop(0, gate_ref.shape[0] // 32, step, 0)


def factors(gate, up):
    tok, ff = gate.shape
    outs = [jax.ShapeDtypeStruct((tok, ff), F32)] * 2
    scratch = [pltpu.VMEM((tok, ff), BF16)] * 2 + [pltpu.SemaphoreType.DMA((2,))]
    return call(factors_body, [pl.ANY] * 2, outs, (gate, up), scratch, 1.0)


def blocks_of(w_down, shards, width, into, sem):
    places = [pl.multiple_of(shard(*which) * width, width) for which in shards]

    def copies(i):
        at = pl.ds(pl.multiple_of(i * TILE, TILE), TILE)
        return [
            pltpu.make_async_copy(
                w_down.at[at, pl.ds(place, width)], into.at[at, pl.ds(j * width, width)], sem.at[i, j]
            )
            for j, place in enumerate(places)
        ]

    return copies


def each(copies, count, what):
    def step(i, carry):
        for copy in copies(i):
            getattr(copy, what)()
        return carry

    lax.fori_loop(0, count, step, 0)


def hidden_body(shards, given, *refs):
    first, held, last, soon, fetch = given
    refs, parts = list(refs), len(shards)
    pieces, w_down, rest = refs[:parts], refs[parts], refs[parts + 1 :]
    before = None if first else rest.pop(0)
    scale = [rest.pop(0), rest.pop(0)] if last else None
    del rest[:soon]
    outs = [rest.pop(0)] + ([rest.pop(0)] if last or fetch else [])
    acts, piece_sem = rest.pop(0), rest.pop(0)
    width = pieces[0].shape[1]
    count = w_down.shape[0] // TILE

    arrivals = [
        pltpu.make_async_copy(piece, acts.at[:, pl.ds(j * width, width)], piece_sem.at[j])
        for j, piece in enumerate(pieces)
    ]
    for copy in arrivals:
        copy.start()
    if held:
        weights = w_down
    else:
        weights, sem = rest.pop(0), rest.pop(0)
        needed = blocks_of(w_down, shards, width, weights, sem)
        each(needed, count, "start")
    if fetch:
        later = blocks_of(w_down, fetch, width, outs[1], rest.pop(0))
        each(later, count, "start")
    for copy in arrivals:
        copy.wait()

    def step(i, carry):
        if not held:
            for copy in needed(i):
                copy.wait()
        at = pl.ds(pl.multiple_of(i * TILE, TILE), TILE)
        total = contract_last(acts[...], weights[at])
        if not first:
            total = total + before[:, at]
        if last:
            for out, factor in zip(outs, scale):
                out[:, at] = (total * factor[:, at]).astype(BF16)
        else:
            outs[0][:, at] = total
        return carry

    lax.fori_loop(0, count, step, 0)
    if fetch:
        each(later, count, "wait")


def hidden(pieces, w_down, total=None, scale=None, soon=(), fetch=(), held=False):
    shards, pieces = zip(*pieces)
    tok, width = pieces[0].shape
    ff = w_down.shape[0]
    parts = len(pieces)
    ins, args = [pl.ANY] * parts + [pltpu.VMEM if held else pl.ANY], (*pieces, w_down)
    if total is not None:
        ins, args = ins + [pltpu.VMEM], (*args, total)
    if scale is not None:
        ins, args = ins + [pltpu.VMEM] * 2, (*args, *scale)
        outs = [jax.ShapeDtypeStruct((tok, ff), BF16)] * 2
    else:
        outs = [jax.ShapeDtypeStruct((tok, ff), F32)]
    ins, args = ins + [pltpu.VMEM] * len(soon), (*args, *soon)
    scratch = [pltpu.VMEM((tok, parts * width), BF16), pltpu.SemaphoreType.DMA((parts,))]
    if not held:
        scratch += [pltpu.VMEM((ff, parts * width), BF16), pltpu.SemaphoreType.DMA((ff // TILE, parts))]
    if fetch:
        outs += [pltpu.VMEM((ff, len(fetch) * width), BF16)]
        scratch += [pltpu.SemaphoreType.DMA((ff // TILE, len(fetch)))]
    given = (total is None, held, scale is not None, len(soon), tuple(fetch))
    return call(functools.partial(hidden_body, shards, given), ins, outs, args, scratch, 3.0)


def partial_sum(block, width, grad_gate, grad_up, w_gate, w_up):
    at = pl.ds(pl.multiple_of(block * width, width), width)
    return contract_last(grad_gate[...], w_gate[at]) + contract_last(grad_up[...], w_up[at])


def each_row(width, body):
    def step(i, carry):
        body(i, pl.ds(pl.multiple_of(i * width, width), width))
        return carry

    lax.fori_loop(0, 2, step, 0)


def sums_body(kept, sent, width, grad_gate, grad_up, w_gate, w_up, *refs):
    given = (grad_gate, grad_up, w_gate, w_up)
    refs = list(refs)
    if kept is not None:
        got, keep, cross = refs.pop(0), refs.pop(0), refs.pop(0)

        def keep_row(i, at):
            total = partial_sum(shard(kept, 1 - i, 0), width, *given) + got[:, at].astype(F32)

            @pl.when(i == 0)
            def _():
                cross[...] = total.astype(BF16)

            @pl.when(i == 1)
            def _():
                keep[...] = total

        each_row(width, keep_row)
    if sent is not None:
        out = refs.pop(0)

        def send_row(i, at):
            out[:, at] = partial_sum(shard(sent, 1 - i, 1), width, *given).astype(BF16)

        each_row(width, send_row)


def sums(grads, weights, width, kept=None, got=None, sent=None):
    tok = grads[0].shape[0]
    args, outs = (*grads, *weights), []
    if kept is not None:
        args = (*args, got)
        outs += [jax.ShapeDtypeStruct((tok, width), F32), jax.ShapeDtypeStruct((tok, width), BF16)]
    if sent is not None:
        outs += [jax.ShapeDtypeStruct((tok, 2 * width), BF16)]
    body = functools.partial(sums_body, kept, sent, width)
    return call(body, [pltpu.VMEM] * len(args), outs, args, [], 1.5 * len(outs) / 2)


def after(x, *earlier):
    return lax.optimization_barrier((x, *earlier))[0]


def staged(grad_out, gate_saved, up_saved, w_gate, w_up, w_down):
    n = 16
    width = grad_out.shape[1]

    def move(x, bits):
        return lax.ppermute(x, "wid", [(i, i ^ bits) for i in range(n)])

    pair, row, near_, mid_ = 1, 2, 4, 8
    half = grad_out.shape[0] // 2
    in_hbm = functools.partial(pltpu.with_memory_space_constraint, memory_space=pltpu.HBM)
    gate_saved, up_saved, w_down = map(in_hbm, (gate_saved, up_saved, w_down))
    weights = [pltpu.with_memory_space_constraint(w, pltpu.VMEM) for w in (w_gate, w_up)]

    scale = factors(gate_saved, up_saved)
    own_row = move(grad_out, row)
    near = move(grad_out, near_)
    mid_a = move(grad_out[:half], mid_)
    own_pair = move(grad_out, pair)

    near = after(near, scale[0])
    near_row = move(near, row)
    mid_b = move(after(grad_out[half:], near), mid_)
    near_pair = move(near, pair)
    own_both = move(own_row, pair)
    (total,) = hidden(
        [((OWN, 0, 0), in_hbm(grad_out)), ((OWN, 0, 1), own_pair), ((OWN, 1, 0), own_row), ((NEAR, 0, 0), near)], w_down
    )

    mid_b, near_row = after(mid_b, total, near_row), after(near_row, mid_b)
    mid = jnp.concatenate([mid_a, mid_b])
    mid_row = move(mid, row)
    far = move(mid, near_)
    mid_pair = move(mid, pair)
    near_both = move(near_row, pair)
    (total,) = hidden(
        [((OWN, 1, 1), own_both), ((NEAR, 0, 1), near_pair), ((NEAR, 1, 0), near_row), ((MID, 0, 0), mid)], w_down, total
    )

    far = after(far, total)
    far_row = move(far, row)
    far_pair = move(far, pair)
    mid_both = move(mid_row, pair)
    last = [(MID, 1, 1), (FAR, 0, 1), (FAR, 1, 0), (FAR, 1, 1)]
    (total,) = hidden(
        [((NEAR, 1, 1), near_both), ((MID, 0, 1), mid_pair), ((MID, 1, 0), mid_row), ((FAR, 0, 0), far)],
        w_down,
        total,
        soon=weights,

    )

    far_row = after(far_row, total)
    far_both = move(far_row, pair)
    grads = hidden(list(zip(last, (mid_both, far_pair, far_row, far_both))), w_down, total, scale)

    step = functools.partial(sums, grads, weights, width)
    (sent_far,) = step(sent=FAR)
    (sent_mid,) = step(sent=MID)
    far, cross_far = step(kept=FAR, got=move(sent_far, pair))
    mid, cross_mid, sent_near = step(kept=MID, got=move(sent_mid, pair), sent=NEAR)
    far = far + move(cross_far, row).astype(F32)

    near, cross_near, sent_own = step(kept=NEAR, got=move(sent_near, pair), sent=OWN)
    mid = mid + after(move(cross_mid, row), cross_near).astype(F32) + move(far.astype(BF16), near_).astype(F32)

    own, cross_own = step(kept=OWN, got=move(sent_own, pair))
    mid = mid.astype(BF16)
    mid_a, near_row = move(mid[:half], mid_), move(cross_near, row)
    mid_a, near_row = after(mid_a, near_row, cross_own), after(near_row, mid_a, cross_own)
    near = near + near_row.astype(F32)

    near = move(near.astype(BF16), near_)
    mid_b = move(mid[half:], mid_)
    own = own + move(cross_own, row).astype(F32) + jnp.concatenate([mid_a, mid_b]).astype(F32)
    return (after(own) + near.astype(F32)).astype(BF16)


def local(grad_out, gate_saved, up_saved, w_gate, w_up, w_down):
    grad_hidden = contract_last(lax.all_gather(grad_out, "wid", axis=1, tiled=True), w_down)
    gate = gate_saved.astype(F32)
    up = up_saved.astype(F32)
    sig = jax.nn.sigmoid(gate)
    grad_gate = (grad_hidden * up * sig * (1.0 + gate * (1.0 - sig))).astype(BF16)
    grad_up = (grad_hidden * gate * sig).astype(BF16)
    summed = lax.psum_scatter(
        contract_last(w_gate, grad_gate) + contract_last(w_up, grad_up),
        "wid",
        scatter_dimension=0,
        tiled=True,
    )
    return summed.astype(BF16).T


def solution(mesh):
    in_specs = (
        P("grp", "wid"),
        P("grp", "wid"),
        P("grp", "wid"),
        P(None, "wid"),
        P(None, "wid"),
        P("wid", None),
    )
    out_specs = P("grp", "wid")
    body = staged if mesh.shape["wid"] == 16 else local
    return jax.shard_map(body, mesh=mesh, in_specs=in_specs, out_specs=out_specs, check_vma=False)
```

```python
import functools

import jax
import jax.numpy as jnp
from jax import lax
from jax.experimental import pallas as pl
from jax.experimental.pallas import tpu as pltpu
from jax.sharding import PartitionSpec as P

BF16, F32 = jnp.bfloat16, jnp.float32
TILE = 256
VMEM = 10 * 2**20
COST = 2e8


def contract_last(left, right):
    return lax.dot_general(
        left, right, (((1,), (1,)), ((), ())), preferred_element_type=F32
    )


OWN, NEAR, MID, FAR = range(4)


def shard(place, row, pair):
    return lax.axis_index("wid") ^ (4 * place + 2 * row + pair)


def call(body, ins, outs, args, scratch, micros):
    return pl.pallas_call(
        body,
        in_specs=[pl.BlockSpec(memory_space=space) for space in ins],
        out_specs=[pl.BlockSpec(memory_space=pltpu.VMEM) for _ in outs],
        out_shape=outs,
        scratch_shapes=scratch,
        compiler_params=pltpu.CompilerParams(vmem_limit_bytes=VMEM),
        cost_estimate=pl.CostEstimate(flops=int(micros * COST), bytes_accessed=0, transcendentals=0),
    )(*args)


def factors_body(gate, up, to_gate_ref, to_up_ref, gate_ref, up_ref, sem):
    copies = [
        pltpu.make_async_copy(source, to, sem.at[k])
        for k, (source, to) in enumerate([(gate, gate_ref), (up, up_ref)])
    ]
    for copy in copies:
        copy.start()
    for copy in copies:
        copy.wait()

    def step(i, carry):
        at = pl.ds(pl.multiple_of(i * 32, 32), 32)
        gate = gate_ref[at].astype(F32)
        up = up_ref[at].astype(F32)
        sig = jax.nn.sigmoid(gate)
        to_gate_ref[at] = up * sig * (1.0 + gate * (1.0 - sig))
        to_up_ref[at] = gate * sig
        return carry

    lax.fori_loop(0, gate_ref.shape[0] // 32, step, 0)


def factors(gate, up):
    tok, ff = gate.shape
    outs = [jax.ShapeDtypeStruct((tok, ff), F32)] * 2
    scratch = [pltpu.VMEM((tok, ff), BF16)] * 2 + [pltpu.SemaphoreType.DMA((2,))]
    return call(factors_body, [pl.ANY] * 2, outs, (gate, up), scratch, 1.0)


def blocks_of(w_down, shards, width, into, sem):
    places = [pl.multiple_of(shard(*which) * width, width) for which in shards]

    def copies(i):
        at = pl.ds(pl.multiple_of(i * TILE, TILE), TILE)
        return [
            pltpu.make_async_copy(
                w_down.at[at, pl.ds(place, width)], into.at[at, pl.ds(j * width, width)], sem.at[i, j]
            )
            for j, place in enumerate(places)
        ]

    return copies


def each(copies, count, what):
    def step(i, carry):
        for copy in copies(i):
            getattr(copy, what)()
        return carry

    lax.fori_loop(0, count, step, 0)


def hidden_body(shards, given, *refs):
    first, held, last, soon, fetch = given
    refs, parts = list(refs), len(shards)
    pieces, w_down, rest = refs[:parts], refs[parts], refs[parts + 1 :]
    before = None if first else rest.pop(0)
    scale = [rest.pop(0), rest.pop(0)] if last else None
    del rest[:soon]
    outs = [rest.pop(0)] + ([rest.pop(0)] if last or fetch else [])
    acts, piece_sem = rest.pop(0), rest.pop(0)
    width = pieces[0].shape[1]
    count = w_down.shape[0] // TILE

    arrivals = [
        pltpu.make_async_copy(piece, acts.at[:, pl.ds(j * width, width)], piece_sem.at[j])
        for j, piece in enumerate(pieces)
    ]
    for copy in arrivals:
        copy.start()
    if held:
        weights = w_down
    else:
        weights, sem = rest.pop(0), rest.pop(0)
        needed = blocks_of(w_down, shards, width, weights, sem)
        each(needed, count, "start")
    if fetch:
        later = blocks_of(w_down, fetch, width, outs[1], rest.pop(0))
        each(later, count, "start")
    for copy in arrivals:
        copy.wait()

    def step(i, carry):
        if not held:
            for copy in needed(i):
                copy.wait()
        at = pl.ds(pl.multiple_of(i * TILE, TILE), TILE)
        total = contract_last(acts[...], weights[at])
        if not first:
            total = total + before[:, at]
        if last:
            for out, factor in zip(outs, scale):
                out[:, at] = (total * factor[:, at]).astype(BF16)
        else:
            outs[0][:, at] = total
        return carry

    lax.fori_loop(0, count, step, 0)
    if fetch:
        each(later, count, "wait")


def hidden(pieces, w_down, total=None, scale=None, soon=(), fetch=(), held=False):
    shards, pieces = zip(*pieces)
    tok, width = pieces[0].shape
    ff = w_down.shape[0]
    parts = len(pieces)
    ins, args = [pl.ANY] * parts + [pltpu.VMEM if held else pl.ANY], (*pieces, w_down)
    if total is not None:
        ins, args = ins + [pltpu.VMEM], (*args, total)
    if scale is not None:
        ins, args = ins + [pltpu.VMEM] * 2, (*args, *scale)
        outs = [jax.ShapeDtypeStruct((tok, ff), BF16)] * 2
    else:
        outs = [jax.ShapeDtypeStruct((tok, ff), F32)]
    ins, args = ins + [pltpu.VMEM] * len(soon), (*args, *soon)
    scratch = [pltpu.VMEM((tok, parts * width), BF16), pltpu.SemaphoreType.DMA((parts,))]
    if not held:
        scratch += [pltpu.VMEM((ff, parts * width), BF16), pltpu.SemaphoreType.DMA((ff // TILE, parts))]
    if fetch:
        outs += [pltpu.VMEM((ff, len(fetch) * width), BF16)]
        scratch += [pltpu.SemaphoreType.DMA((ff // TILE, len(fetch)))]
    given = (total is None, held, scale is not None, len(soon), tuple(fetch))
    return call(functools.partial(hidden_body, shards, given), ins, outs, args, scratch, 3.0)


def partial_sum(block, width, grad_gate, grad_up, w_gate, w_up):
    at = pl.ds(pl.multiple_of(block * width, width), width)
    return contract_last(grad_gate[...], w_gate[at]) + contract_last(grad_up[...], w_up[at])


def each_row(width, body):
    def step(i, carry):
        body(i, pl.ds(pl.multiple_of(i * width, width), width))
        return carry

    lax.fori_loop(0, 2, step, 0)


def sums_body(kept, arrived, sent, width, grad_gate, grad_up, w_gate, w_up, *refs):
    given = (grad_gate, grad_up, w_gate, w_up)
    refs = list(refs)
    if kept is not None:
        got = refs.pop(0) if arrived else None
        keep, cross = refs.pop(0), refs.pop(0)

        def keep_row(i, at):
            total = partial_sum(shard(kept, 1 - i, 0), width, *given)
            if arrived:
                total = total + got[:, at].astype(F32)

            @pl.when(i == 0)
            def _():
                cross[...] = total.astype(cross.dtype)

            @pl.when(i == 1)
            def _():
                keep[...] = total

        each_row(width, keep_row)
    if sent is not None:
        out = refs.pop(0)

        def send_row(i, at):
            out[:, at] = partial_sum(shard(sent, 1 - i, 1), width, *given).astype(BF16)

        each_row(width, send_row)


def sums(grads, weights, width, kept=None, got=None, sent=None):
    tok = grads[0].shape[0]
    args, outs = (*grads, *weights), []
    if kept is not None:
        args = args if got is None else (*args, got)
        outs += [jax.ShapeDtypeStruct((tok, width), dtype) for dtype in (F32, F32 if got is None else BF16)]
    if sent is not None:
        outs += [jax.ShapeDtypeStruct((tok, 2 * width), BF16)]
    body = functools.partial(sums_body, kept, got is not None, sent, width)
    return call(body, [pltpu.VMEM] * len(args), outs, args, [], 1.5 * len(outs) / 2)


def after(x, *earlier):
    return lax.optimization_barrier((x, *earlier))[0]


def staged(grad_out, gate_saved, up_saved, w_gate, w_up, w_down):
    n = 16
    width = grad_out.shape[1]

    def move(x, bits):
        return lax.ppermute(x, "wid", [(i, i ^ bits) for i in range(n)])

    pair, row, near_, mid_ = 1, 2, 4, 8
    half = grad_out.shape[0] // 2
    in_hbm = functools.partial(pltpu.with_memory_space_constraint, memory_space=pltpu.HBM)
    gate_saved, up_saved, w_down = map(in_hbm, (gate_saved, up_saved, w_down))
    weights = [pltpu.with_memory_space_constraint(w, pltpu.VMEM) for w in (w_gate, w_up)]

    scale = factors(gate_saved, up_saved)
    own_row = move(grad_out, row)
    near = move(grad_out, near_)
    mid = move(grad_out, mid_)
    own_pair = move(grad_out, pair)

    near = after(near, scale[0])
    near_row = move(near, row)
    near_pair = move(near, pair)
    own_both = move(own_row, pair)
    (total,) = hidden(
        [((OWN, 0, 0), in_hbm(grad_out)), ((OWN, 0, 1), own_pair), ((OWN, 1, 0), own_row), ((NEAR, 0, 0), near)], w_down
    )

    mid = after(mid, total)
    mid_row = move(mid, row)
    far = move(mid, near_)
    mid_pair = move(mid, pair)
    near_both = move(near_row, pair)
    (total,) = hidden(
        [((OWN, 1, 1), own_both), ((NEAR, 0, 1), near_pair), ((NEAR, 1, 0), near_row), ((MID, 0, 0), mid)], w_down, total
    )

    far = after(far, total)
    far_row = move(far, row)
    far_pair = move(far, pair)
    mid_both = move(mid_row, pair)
    last = [(MID, 1, 1), (FAR, 0, 1), (FAR, 1, 0), (FAR, 1, 1)]
    (total,) = hidden(
        [((NEAR, 1, 1), near_both), ((MID, 0, 1), mid_pair), ((MID, 1, 0), mid_row), ((FAR, 0, 0), far)],
        w_down,
        total,
        soon=weights,

    )

    far_row = after(far_row, total)
    far_both = move(far_row, pair)
    grads = hidden(list(zip(last, (mid_both, far_pair, far_row, far_both))), w_down, total, scale)

    step = functools.partial(sums, grads, weights, width)
    (sent_far,) = step(sent=FAR)
    far, cross_far = step(kept=FAR)
    got_far = move(sent_far, pair).astype(F32)
    far, cross_far = far + got_far[:, width:], (cross_far + got_far[:, :width]).astype(BF16)
    (sent_mid,) = sums([after(grad, cross_far) for grad in grads], weights, width, sent=MID)
    mid, cross_mid, sent_near = step(kept=MID, got=move(sent_mid, pair), sent=NEAR)
    far = far + move(cross_far, row).astype(F32)

    near, cross_near, sent_own = step(kept=NEAR, got=move(sent_near, pair), sent=OWN)
    mid = mid + after(move(cross_mid, row), cross_near).astype(F32) + move(far.astype(BF16), near_).astype(F32)

    own, cross_own = step(kept=OWN, got=move(sent_own, pair))
    mid = mid.astype(BF16)
    mid_a, near_row = move(mid[:half], mid_), move(cross_near, row)
    mid_a, near_row = after(mid_a, near_row, cross_own), after(near_row, mid_a, cross_own)
    near = near + near_row.astype(F32)

    near = move(near.astype(BF16), near_)
    mid_b = move(mid[half:], mid_)
    own = own + move(cross_own, row).astype(F32) + jnp.concatenate([mid_a, mid_b]).astype(F32)
    return (after(own) + near.astype(F32)).astype(BF16)


def local(grad_out, gate_saved, up_saved, w_gate, w_up, w_down):
    grad_hidden = contract_last(lax.all_gather(grad_out, "wid", axis=1, tiled=True), w_down)
    gate = gate_saved.astype(F32)
    up = up_saved.astype(F32)
    sig = jax.nn.sigmoid(gate)
    grad_gate = (grad_hidden * up * sig * (1.0 + gate * (1.0 - sig))).astype(BF16)
    grad_up = (grad_hidden * gate * sig).astype(BF16)
    summed = lax.psum_scatter(
        contract_last(w_gate, grad_gate) + contract_last(w_up, grad_up),
        "wid",
        scatter_dimension=0,
        tiled=True,
    )
    return summed.astype(BF16).T


def solution(mesh):
    in_specs = (
        P("grp", "wid"),
        P("grp", "wid"),
        P("grp", "wid"),
        P(None, "wid"),
        P(None, "wid"),
        P("wid", None),
    )
    out_specs = P("grp", "wid")
    body = staged if mesh.shape["wid"] == 16 else local
    return jax.shard_map(body, mesh=mesh, in_specs=in_specs, out_specs=out_specs, check_vma=False)
```

```python
import functools

import jax
import jax.numpy as jnp
from jax import lax
from jax.experimental import pallas as pl
from jax.experimental.pallas import tpu as pltpu
from jax.sharding import PartitionSpec as P

BF16, F32 = jnp.bfloat16, jnp.float32
TILE = 256
VMEM = 7 * 2**20
COST = 5e7


def contract_last(left, right):
    return lax.dot_general(
        left, right, (((1,), (1,)), ((), ())), preferred_element_type=F32
    )


OWN, NEAR, MID, FAR = range(4)


def shard(place, row, pair):
    return lax.axis_index("wid") ^ (4 * place + 2 * row + pair)


def call(body, ins, outs, args, scratch, micros):
    return pl.pallas_call(
        body,
        in_specs=[pl.BlockSpec(memory_space=space) for space in ins],
        out_specs=[pl.BlockSpec(memory_space=pltpu.VMEM) for _ in outs],
        out_shape=outs,
        scratch_shapes=scratch,
        compiler_params=pltpu.CompilerParams(vmem_limit_bytes=VMEM),
        cost_estimate=pl.CostEstimate(flops=int(micros * COST), bytes_accessed=0, transcendentals=0),
    )(*args)


def factors_body(gate, up, to_gate_ref, to_up_ref, gate_ref, up_ref, sem):
    copies = [
        pltpu.make_async_copy(source, to, sem.at[k])
        for k, (source, to) in enumerate([(gate, gate_ref), (up, up_ref)])
    ]
    for copy in copies:
        copy.start()
    for copy in copies:
        copy.wait()

    def step(i, carry):
        at = pl.ds(pl.multiple_of(i * 32, 32), 32)
        gate = gate_ref[at].astype(F32)
        up = up_ref[at].astype(F32)
        sig = jax.nn.sigmoid(gate)
        to_gate_ref[at] = up * sig * (1.0 + gate * (1.0 - sig))
        to_up_ref[at] = gate * sig
        return carry

    lax.fori_loop(0, gate_ref.shape[0] // 32, step, 0)


def factors(gate, up):
    tok, ff = gate.shape
    outs = [jax.ShapeDtypeStruct((tok, ff), F32)] * 2
    scratch = [pltpu.VMEM((tok, ff), BF16)] * 2 + [pltpu.SemaphoreType.DMA((2,))]
    return call(factors_body, [pl.ANY] * 2, outs, (gate, up), scratch, 1.0)


def blocks_of(w_down, shards, width, into, sem):
    places = [pl.multiple_of(shard(*which) * width, width) for which in shards]

    def copies(i):
        at = pl.ds(pl.multiple_of(i * TILE, TILE), TILE)
        return [
            pltpu.make_async_copy(
                w_down.at[at, pl.ds(place, width)], into.at[at, pl.ds(j * width, width)], sem.at[i, j]
            )
            for j, place in enumerate(places)
        ]

    return copies


def each(copies, count, what):
    def step(i, carry):
        for copy in copies(i):
            getattr(copy, what)()
        return carry

    lax.fori_loop(0, count, step, 0)


def hidden_body(shards, given, *refs):
    first, held, last, fetch = given
    refs, parts = list(refs), len(shards)
    pieces, w_down, rest = refs[:parts], refs[parts], refs[parts + 1 :]
    before = None if first else rest.pop(0)
    scale = [rest.pop(0), rest.pop(0)] if last else None
    outs = [rest.pop(0)] + ([rest.pop(0)] if last or fetch else [])
    acts, piece_sem = rest.pop(0), rest.pop(0)
    width = pieces[0].shape[1]
    count = w_down.shape[0] // TILE

    arrivals = [
        pltpu.make_async_copy(piece, acts.at[:, pl.ds(j * width, width)], piece_sem.at[j])
        for j, piece in enumerate(pieces)
    ]
    for copy in arrivals:
        copy.start()
    if held:
        weights = w_down
    else:
        weights, sem = rest.pop(0), rest.pop(0)
        needed = blocks_of(w_down, shards, width, weights, sem)
        each(needed, count, "start")
    if fetch:
        later = blocks_of(w_down, fetch, width, outs[1], rest.pop(0))
        each(later, count, "start")
    for copy in arrivals:
        copy.wait()

    def step(i, carry):
        if not held:
            for copy in needed(i):
                copy.wait()
        at = pl.ds(pl.multiple_of(i * TILE, TILE), TILE)
        total = contract_last(acts[...], weights[at])
        if not first:
            total = total + before[:, at]
        if last:
            for out, factor in zip(outs, scale):
                out[:, at] = (total * factor[:, at]).astype(BF16)
        else:
            outs[0][:, at] = total
        return carry

    lax.fori_loop(0, count, step, 0)
    if fetch:
        each(later, count, "wait")


def hidden(pieces, w_down, total=None, scale=None, fetch=(), held=False):
    shards, pieces = zip(*pieces)
    tok, width = pieces[0].shape
    ff = w_down.shape[0]
    parts = len(pieces)
    ins, args = [pl.ANY] * parts + [pltpu.VMEM if held else pl.ANY], (*pieces, w_down)
    if total is not None:
        ins, args = ins + [pltpu.VMEM], (*args, total)
    if scale is not None:
        ins, args = ins + [pltpu.VMEM] * 2, (*args, *scale)
        outs = [jax.ShapeDtypeStruct((tok, ff), BF16)] * 2
    else:
        outs = [jax.ShapeDtypeStruct((tok, ff), F32)]
    scratch = [pltpu.VMEM((tok, parts * width), BF16), pltpu.SemaphoreType.DMA((parts,))]
    if not held:
        scratch += [pltpu.VMEM((ff, parts * width), BF16), pltpu.SemaphoreType.DMA((ff // TILE, parts))]
    if fetch:
        outs += [pltpu.VMEM((ff, len(fetch) * width), BF16)]
        scratch += [pltpu.SemaphoreType.DMA((ff // TILE, len(fetch)))]
    given = (total is None, held, scale is not None, tuple(fetch))
    return call(functools.partial(hidden_body, shards, given), ins, outs, args, scratch, 3.0)


def partial_sum(block, width, grad_gate, grad_up, w_gate, w_up):
    at = pl.ds(pl.multiple_of(block * width, width), width)
    return contract_last(grad_gate[...], w_gate[at]) + contract_last(grad_up[...], w_up[at])


def each_row(width, body):
    def step(i, carry):
        body(i, pl.ds(pl.multiple_of(i * width, width), width))
        return carry

    lax.fori_loop(0, 2, step, 0)


def sums_body(kept, arrived, sent, width, grad_gate, grad_up, w_gate, w_up, *refs):
    given = (grad_gate, grad_up, w_gate, w_up)
    refs = list(refs)
    if kept is not None:
        got = refs.pop(0) if arrived else None
        keep, cross = refs.pop(0), refs.pop(0)

        def keep_row(i, at):
            total = partial_sum(shard(kept, 1 - i, 0), width, *given)
            if arrived:
                total = total + got[:, at].astype(F32)

            @pl.when(i == 0)
            def _():
                cross[...] = total.astype(cross.dtype)

            @pl.when(i == 1)
            def _():
                keep[...] = total

        each_row(width, keep_row)
    if sent is not None:
        out = refs.pop(0)

        def send_row(i, at):
            out[:, at] = partial_sum(shard(sent, 1 - i, 1), width, *given).astype(BF16)

        each_row(width, send_row)


def sums(grads, weights, width, kept=None, got=None, sent=None):
    tok = grads[0].shape[0]
    args, outs = (*grads, *weights), []
    if kept is not None:
        args = args if got is None else (*args, got)
        outs += [jax.ShapeDtypeStruct((tok, width), dtype) for dtype in (F32, F32 if got is None else BF16)]
    if sent is not None:
        outs += [jax.ShapeDtypeStruct((tok, 2 * width), BF16)]
    body = functools.partial(sums_body, kept, got is not None, sent, width)
    return call(body, [pltpu.VMEM] * len(args), outs, args, [], 1.5 * len(outs) / 2)


def after(x, *earlier):
    return lax.optimization_barrier((x, *earlier))[0]


def staged(grad_out, gate_saved, up_saved, w_gate, w_up, w_down):
    n = 16
    width = grad_out.shape[1]

    def move(x, bits):
        return lax.ppermute(x, "wid", [(i, i ^ bits) for i in range(n)])

    pair, row, near_, mid_ = 1, 2, 4, 8
    half = grad_out.shape[0] // 2
    in_hbm = functools.partial(pltpu.with_memory_space_constraint, memory_space=pltpu.HBM)
    gate_saved, up_saved, w_down = map(in_hbm, (gate_saved, up_saved, w_down))
    weights = [pltpu.with_memory_space_constraint(w, pltpu.VMEM) for w in (w_gate, w_up)]

    scale = factors(gate_saved, up_saved)
    own_row = move(grad_out, row)
    near = move(grad_out, near_)
    mid = move(grad_out, mid_)
    own_pair = move(grad_out, pair)

    near = after(near, scale[0])
    near_row = move(near, row)
    near_pair = move(near, pair)
    own_both = move(own_row, pair)
    (total,) = hidden(
        [((OWN, 0, 0), in_hbm(grad_out)), ((OWN, 0, 1), own_pair), ((OWN, 1, 0), own_row), ((NEAR, 0, 0), near)], w_down
    )

    mid = after(mid, total)
    mid_row = move(mid, row)
    far = move(mid, near_)
    mid_pair = move(mid, pair)
    near_both = move(near_row, pair)
    (total,) = hidden(
        [((OWN, 1, 1), own_both), ((NEAR, 0, 1), near_pair), ((NEAR, 1, 0), near_row), ((MID, 0, 0), mid)], w_down, total
    )

    far = after(far, total)
    far_row = move(far, row)
    far_pair = move(far, pair)
    mid_both = move(mid_row, pair)
    last = [(MID, 1, 1), (FAR, 0, 1), (FAR, 1, 0), (FAR, 1, 1)]
    total, held = hidden(
        [((NEAR, 1, 1), near_both), ((MID, 0, 1), mid_pair), ((MID, 1, 0), mid_row), ((FAR, 0, 0), far)],
        w_down,
        total,
        fetch=last,
    )

    far_row = after(far_row, total)
    far_both = move(far_row, pair)
    grads = hidden(list(zip(last, (mid_both, far_pair, far_row, far_both))), held, total, scale, held=True)

    step = functools.partial(sums, grads, weights, width)
    (sent_far,) = step(sent=FAR)
    far, cross_far = step(kept=FAR)
    got_far = move(sent_far, pair).astype(F32)
    far, cross_far = far + got_far[:, width:], (cross_far + got_far[:, :width]).astype(BF16)
    (sent_mid,) = sums([after(grad, cross_far) for grad in grads], weights, width, sent=MID)
    mid, cross_mid, sent_near = step(kept=MID, got=move(sent_mid, pair), sent=NEAR)
    far = far + move(cross_far, row).astype(F32)

    near, cross_near, sent_own = step(kept=NEAR, got=move(sent_near, pair), sent=OWN)
    mid = mid + after(move(cross_mid, row), cross_near).astype(F32) + move(far.astype(BF16), near_).astype(F32)

    own, cross_own = step(kept=OWN, got=move(sent_own, pair))
    mid = mid.astype(BF16)
    mid_a, near_row = move(mid[:half], mid_), move(cross_near, row)
    mid_a, near_row = after(mid_a, near_row, cross_own), after(near_row, mid_a, cross_own)
    near = near + near_row.astype(F32)

    near = move(near.astype(BF16), near_)
    mid_b = move(mid[half:], mid_)
    own = own + move(cross_own, row).astype(F32) + jnp.concatenate([mid_a, mid_b]).astype(F32)
    return (after(own) + near.astype(F32)).astype(BF16)


def local(grad_out, gate_saved, up_saved, w_gate, w_up, w_down):
    grad_hidden = contract_last(lax.all_gather(grad_out, "wid", axis=1, tiled=True), w_down)
    gate = gate_saved.astype(F32)
    up = up_saved.astype(F32)
    sig = jax.nn.sigmoid(gate)
    grad_gate = (grad_hidden * up * sig * (1.0 + gate * (1.0 - sig))).astype(BF16)
    grad_up = (grad_hidden * gate * sig).astype(BF16)
    summed = lax.psum_scatter(
        contract_last(w_gate, grad_gate) + contract_last(w_up, grad_up),
        "wid",
        scatter_dimension=0,
        tiled=True,
    )
    return summed.astype(BF16).T


def solution(mesh):
    in_specs = (
        P("grp", "wid"),
        P("grp", "wid"),
        P("grp", "wid"),
        P(None, "wid"),
        P(None, "wid"),
        P("wid", None),
    )
    out_specs = P("grp", "wid")
    body = staged if mesh.shape["wid"] == 16 else local
    return jax.shard_map(body, mesh=mesh, in_specs=in_specs, out_specs=out_specs, check_vma=False)
```

```python
import functools

import jax
import jax.numpy as jnp
from jax import lax
from jax.experimental import pallas as pl
from jax.experimental.pallas import tpu as pltpu
from jax.sharding import PartitionSpec as P

BF16, F32 = jnp.bfloat16, jnp.float32
TILE = 256
VMEM = 7 * 2**20
COST = 5e7


def contract_last(left, right):
    return lax.dot_general(
        left, right, (((1,), (1,)), ((), ())), preferred_element_type=F32
    )


OWN, NEAR, MID, FAR = range(4)


def shard(place, row, pair):
    return lax.axis_index("wid") ^ (4 * place + 2 * row + pair)


def call(body, ins, outs, args, scratch, micros):
    return pl.pallas_call(
        body,
        in_specs=[pl.BlockSpec(memory_space=space) for space in ins],
        out_specs=[pl.BlockSpec(memory_space=pltpu.VMEM) for _ in outs],
        out_shape=outs,
        scratch_shapes=scratch,
        compiler_params=pltpu.CompilerParams(vmem_limit_bytes=VMEM),
        cost_estimate=pl.CostEstimate(flops=int(micros * COST), bytes_accessed=0, transcendentals=0),
    )(*args)


def factors_body(gate, up, to_gate_ref, to_up_ref, gate_ref, up_ref, sem):
    copies = [
        pltpu.make_async_copy(source, to, sem.at[k])
        for k, (source, to) in enumerate([(gate, gate_ref), (up, up_ref)])
    ]
    for copy in copies:
        copy.start()
    for copy in copies:
        copy.wait()

    def step(i, carry):
        at = pl.ds(pl.multiple_of(i * 32, 32), 32)
        gate = gate_ref[at].astype(F32)
        up = up_ref[at].astype(F32)
        sig = jax.nn.sigmoid(gate)
        to_gate_ref[at] = up * sig * (1.0 + gate * (1.0 - sig))
        to_up_ref[at] = gate * sig
        return carry

    lax.fori_loop(0, gate_ref.shape[0] // 32, step, 0)


def factors(gate, up):
    tok, ff = gate.shape
    outs = [jax.ShapeDtypeStruct((tok, ff), F32)] * 2
    scratch = [pltpu.VMEM((tok, ff), BF16)] * 2 + [pltpu.SemaphoreType.DMA((2,))]
    return call(factors_body, [pl.ANY] * 2, outs, (gate, up), scratch, 1.0)


def blocks_of(w_down, shards, width, into, sem):
    places = [pl.multiple_of(shard(*which) * width, width) for which in shards]

    def copies(i):
        at = pl.ds(pl.multiple_of(i * TILE, TILE), TILE)
        return [
            pltpu.make_async_copy(
                w_down.at[at, pl.ds(place, width)], into.at[at, pl.ds(j * width, width)], sem.at[i, j]
            )
            for j, place in enumerate(places)
        ]

    return copies


def each(copies, count, what):
    def step(i, carry):
        for copy in copies(i):
            getattr(copy, what)()
        return carry

    lax.fori_loop(0, count, step, 0)


def hidden_body(shards, given, *refs):
    first, held, last, fetch = given
    refs, parts = list(refs), len(shards)
    pieces, w_down, rest = refs[:parts], refs[parts], refs[parts + 1 :]
    before = None if first else rest.pop(0)
    scale = [rest.pop(0), rest.pop(0)] if last else None
    outs = [rest.pop(0)] + ([rest.pop(0)] if last or fetch else [])
    acts, piece_sem = rest.pop(0), rest.pop(0)
    width = pieces[0].shape[1]
    count = w_down.shape[0] // TILE

    arrivals = [
        pltpu.make_async_copy(piece, acts.at[:, pl.ds(j * width, width)], piece_sem.at[j])
        for j, piece in enumerate(pieces)
    ]
    for copy in arrivals:
        copy.start()
    if held:
        weights = w_down
    else:
        weights, sem = rest.pop(0), rest.pop(0)
        needed = blocks_of(w_down, shards, width, weights, sem)
        each(needed, count, "start")
    if fetch:
        later = blocks_of(w_down, fetch, width, outs[1], rest.pop(0))
        each(later, count, "start")
    for copy in arrivals:
        copy.wait()

    def step(i, carry):
        if not held:
            for copy in needed(i):
                copy.wait()
        at = pl.ds(pl.multiple_of(i * TILE, TILE), TILE)
        total = contract_last(acts[...], weights[at])
        if not first:
            total = total + before[:, at]
        if last:
            for out, factor in zip(outs, scale):
                out[:, at] = (total * factor[:, at]).astype(BF16)
        else:
            outs[0][:, at] = total
        return carry

    lax.fori_loop(0, count, step, 0)
    if fetch:
        each(later, count, "wait")


def hidden(pieces, w_down, total=None, scale=None, fetch=(), held=False):
    shards, pieces = zip(*pieces)
    tok, width = pieces[0].shape
    ff = w_down.shape[0]
    parts = len(pieces)
    ins, args = [pl.ANY] * parts + [pltpu.VMEM if held else pl.ANY], (*pieces, w_down)
    if total is not None:
        ins, args = ins + [pltpu.VMEM], (*args, total)
    if scale is not None:
        ins, args = ins + [pltpu.VMEM] * 2, (*args, *scale)
        outs = [jax.ShapeDtypeStruct((tok, ff), BF16)] * 2
    else:
        outs = [jax.ShapeDtypeStruct((tok, ff), F32)]
    scratch = [pltpu.VMEM((tok, parts * width), BF16), pltpu.SemaphoreType.DMA((parts,))]
    if not held:
        scratch += [pltpu.VMEM((ff, parts * width), BF16), pltpu.SemaphoreType.DMA((ff // TILE, parts))]
    if fetch:
        outs += [pltpu.VMEM((ff, len(fetch) * width), BF16)]
        scratch += [pltpu.SemaphoreType.DMA((ff // TILE, len(fetch)))]
    given = (total is None, held, scale is not None, tuple(fetch))
    return call(functools.partial(hidden_body, shards, given), ins, outs, args, scratch, 3.0)


def partial_sum(block, width, grad_gate, grad_up, w_gate, w_up):
    at = pl.ds(pl.multiple_of(block * width, width), width)
    return contract_last(grad_gate[...], w_gate[at]) + contract_last(grad_up[...], w_up[at])


def each_row(width, body):
    def step(i, carry):
        body(i, pl.ds(pl.multiple_of(i * width, width), width))
        return carry

    lax.fori_loop(0, 2, step, 0)


def sums_body(kept, arrived, sent, width, grad_gate, grad_up, w_gate, w_up, *refs):
    given = (grad_gate, grad_up, w_gate, w_up)
    refs = list(refs)
    if kept is not None:
        got = refs.pop(0) if arrived else None
        keep, cross = refs.pop(0), refs.pop(0)

        def keep_row(i, at):
            total = partial_sum(shard(kept, 1 - i, 0), width, *given)
            if arrived:
                total = total + got[:, at].astype(F32)

            @pl.when(i == 0)
            def _():
                cross[...] = total.astype(cross.dtype)

            @pl.when(i == 1)
            def _():
                keep[...] = total

        each_row(width, keep_row)
    if sent is not None:
        out = refs.pop(0)

        def send_row(i, at):
            out[:, at] = partial_sum(shard(sent, 1 - i, 1), width, *given).astype(BF16)

        each_row(width, send_row)


def sums(grads, weights, width, kept=None, got=None, sent=None):
    tok = grads[0].shape[0]
    args, outs = (*grads, *weights), []
    if kept is not None:
        args = args if got is None else (*args, got)
        outs += [jax.ShapeDtypeStruct((tok, width), dtype) for dtype in (F32, F32 if got is None else BF16)]
    if sent is not None:
        outs += [jax.ShapeDtypeStruct((tok, 2 * width), BF16)]
    body = functools.partial(sums_body, kept, got is not None, sent, width)
    return call(body, [pltpu.VMEM] * len(args), outs, args, [], 1.5 * len(outs) / 2)


def after(x, *earlier):
    return lax.optimization_barrier((x, *earlier))[0]


def staged(grad_out, gate_saved, up_saved, w_gate, w_up, w_down):
    n = 16
    width = grad_out.shape[1]

    def move(x, bits):
        return lax.ppermute(x, "wid", [(i, i ^ bits) for i in range(n)])

    pair, row, near_, mid_ = 1, 2, 4, 8
    half = grad_out.shape[0] // 2
    in_hbm = functools.partial(pltpu.with_memory_space_constraint, memory_space=pltpu.HBM)
    gate_saved, up_saved, w_down = map(in_hbm, (gate_saved, up_saved, w_down))
    weights = [pltpu.with_memory_space_constraint(w, pltpu.VMEM) for w in (w_gate, w_up)]

    scale = factors(gate_saved, up_saved)
    own_row = move(grad_out, row)
    near = move(grad_out, near_)
    mid = move(grad_out, mid_)
    own_pair = move(grad_out, pair)

    near = after(near, scale[0])
    near_row = move(near, row)
    near_pair = move(near, pair)
    own_both = move(own_row, pair)
    (total,) = hidden(
        [((OWN, 0, 0), in_hbm(grad_out)), ((OWN, 0, 1), own_pair), ((OWN, 1, 0), own_row), ((NEAR, 0, 0), near)], w_down
    )

    mid = after(mid, total)
    mid_row = move(mid, row)
    far = move(mid, near_)
    mid_pair = move(mid, pair)
    near_both = move(near_row, pair)
    (total,) = hidden(
        [((OWN, 1, 1), own_both), ((NEAR, 0, 1), near_pair), ((NEAR, 1, 0), near_row), ((MID, 0, 0), mid)], w_down, total
    )

    far = after(far, total)
    far_row = move(far, row)
    far_pair = move(far, pair)
    mid_both = move(mid_row, pair)
    last = [(MID, 1, 1), (FAR, 0, 1), (FAR, 1, 0), (FAR, 1, 1)]
    total, held = hidden(
        [((NEAR, 1, 1), near_both), ((MID, 0, 1), mid_pair), ((MID, 1, 0), mid_row), ((FAR, 0, 0), far)],
        w_down,
        total,
        fetch=last,
    )

    far_row = after(far_row, total)
    far_both = move(far_row, pair)
    grads = hidden(list(zip(last, (mid_both, far_pair, far_row, far_both))), held, total, scale, held=True)

    step = functools.partial(sums, grads, weights, width)
    (sent_far,) = step(sent=FAR)
    far, cross_far = step(kept=FAR)
    got_far = move(sent_far, pair)
    far, cross_far = far + got_far[:, width:].astype(F32), (cross_far + got_far[:, :width].astype(F32)).astype(BF16)
    (sent_mid,) = sums([after(grad, cross_far) for grad in grads], weights, width, sent=MID)
    mid, cross_mid, sent_near = step(kept=MID, got=move(sent_mid, pair), sent=NEAR)
    far = far + move(cross_far, row).astype(F32)

    near, cross_near, sent_own = step(kept=NEAR, got=move(sent_near, pair), sent=OWN)
    mid = mid + after(move(cross_mid, row), cross_near).astype(F32) + move(far.astype(BF16), near_).astype(F32)

    own, cross_own = step(kept=OWN, got=move(sent_own, pair))
    mid = mid.astype(BF16)
    mid_a, near_row = move(mid[:half], mid_), move(cross_near, row)
    mid_a, near_row = after(mid_a, near_row, cross_own), after(near_row, mid_a, cross_own)
    near = near + near_row.astype(F32)

    near = move(near.astype(BF16), near_)
    mid_b = move(mid[half:], mid_)
    own = own + move(cross_own, row).astype(F32) + jnp.concatenate([mid_a, mid_b]).astype(F32)
    return (after(own) + near.astype(F32)).astype(BF16)


def local(grad_out, gate_saved, up_saved, w_gate, w_up, w_down):
    grad_hidden = contract_last(lax.all_gather(grad_out, "wid", axis=1, tiled=True), w_down)
    gate = gate_saved.astype(F32)
    up = up_saved.astype(F32)
    sig = jax.nn.sigmoid(gate)
    grad_gate = (grad_hidden * up * sig * (1.0 + gate * (1.0 - sig))).astype(BF16)
    grad_up = (grad_hidden * gate * sig).astype(BF16)
    summed = lax.psum_scatter(
        contract_last(w_gate, grad_gate) + contract_last(w_up, grad_up),
        "wid",
        scatter_dimension=0,
        tiled=True,
    )
    return summed.astype(BF16).T


def solution(mesh):
    in_specs = (
        P("grp", "wid"),
        P("grp", "wid"),
        P("grp", "wid"),
        P(None, "wid"),
        P(None, "wid"),
        P("wid", None),
    )
    out_specs = P("grp", "wid")
    body = staged if mesh.shape["wid"] == 16 else local
    return jax.shard_map(body, mesh=mesh, in_specs=in_specs, out_specs=out_specs, check_vma=False)
```
